128 devices in a mesh: rep: 16 (over z, x_lo, core), shard: 8 (over y, x_hi).
Axes of the slice: x: 4 (x_hi: 2, x_lo: 2; x = x_hi * 2 + x_lo), y: 4, z: 4, core: 2. Of those that a mesh axis runs over, the one named last changes fastest.
Arguments:
- tokens: bfloat16 [32768, 1024], P(('rep', 'shard')), may hold values from -6 to 6
- norm_in: bfloat16 [1024], P('shard'), may hold values from 0.5 to 1.5
- w_query: bfloat16 [1024, 1024], P('shard'), may hold values from -0.1875 to 0.1875
- w_key: bfloat16 [1024, 1024], P('shard'), may hold values from -0.1875 to 0.1875
- w_value: bfloat16 [1024, 2048], P('shard'), may hold values from -0.1875 to 0.1875
- w_gate_out: bfloat16 [1024, 2048], P('shard'), may hold values from -0.1875 to 0.1875
- w_decay: bfloat16 [1024, 8], P('shard'), may hold values from -0.1875 to 0.1875
- w_beta: bfloat16 [1024, 8], P('shard'), may hold values from -0.1875 to 0.1875
- decay_log: bfloat16 [8], P('shard'), may hold values from -6 to -1
- decay_bias: bfloat16 [8], P('shard'), may hold values from -2 to 1
- conv_weight: bfloat16 [4, 4096], P(None, 'shard'), may hold values from -2 to 2
- head_gain: bfloat16 [256], P('shard'), may hold values from 0.5 to 1.5
- w_output: bfloat16 [2048, 1024], P('shard'), may hold values from -0.125 to 0.125
- norm_mid: bfloat16 [1024], P('shard'), may hold values from 0.5 to 1.5
- w_gate: bfloat16 [1024, 2816], P('shard'), may hold values from -0.1875 to 0.1875
- w_up: bfloat16 [1024, 2816], P('shard'), may hold values from -0.1875 to 0.1875
- w_down: bfloat16 [2816, 1024], P('shard'), may hold values from -0.109375 to 0.109375
- lengths: int32 [128], P(('rep', 'shard')), may hold values from 64 to 256, as said below
- cotangent: bfloat16 [32768, 1024], P(('rep', 'shard')), may hold values from -6 to 6
Outputs:
- block_out: bfloat16 [32768, 1024], P(('rep', 'shard'))
- input_grad: float32 [32768, 1024], P(('rep', 'shard'))
- grad_norm_in: float32 [1024], P('shard')
- grad_query: float32 [1024, 1024], P('shard')
- grad_key: float32 [1024, 1024], P('shard')
- grad_value: float32 [1024, 2048], P('shard')
- grad_gate_out: float32 [1024, 2048], P('shard')
- grad_decay: float32 [1024, 8], P('shard')
- grad_beta: float32 [1024, 8], P('shard')
- grad_decay_log: float32 [8], P('shard')
- grad_decay_bias: float32 [8], P('shard')
- grad_conv: float32 [4, 4096], P(None, 'shard')
- grad_head_gain: float32 [256], P('shard')
- grad_output: float32 [2048, 1024], P('shard')
- grad_norm_mid: float32 [1024], P('shard')
- grad_gate: float32 [1024, 2816], P('shard')
- grad_up: float32 [1024, 2816], P('shard')
- grad_down: float32 [2816, 1024], P('shard')
The draws below stay inside these ranges and needn't reach their ends.
Inputs may be any that keep to these rules, and one draw needn't show every extreme that they name: Each device's sequence occupies the first lengths entries of its 256 slots; some sequence fills all 256 slots and some has 64 live tokens.
All inputs are finite; a program needn't handle non-finite values.
Results may differ from the reference program's by a relative error of at most 0.0098.
Values may be sent and summed in bfloat16 or wider, within the bound.
No kernel may reach another device: no remote copies, remote signals or barrier semaphores. Data moves between devices by JAX's collectives and lax.ppermute only.
A program may use at most 256 MiB of HBM per device.

```python
import jax
import jax.numpy as jnp
from jax import lax

D = 1024
NH = 8
DK = 128
DV = 256
FF = 2816
CONV = 4
SPAN = 64
TOK_DEV = 256
KDIM = 1024
VDIM = 2048
CH = 4096
SEQS = 128
TOKENS = 32768


def draw_lengths(key, part):
    key = jax.random.fold_in(key, 17)
    first, second = jax.random.split(key)
    drawn = jax.random.randint(first, (SEQS,), TOK_DEV // 4, TOK_DEV + 1)
    order = jax.random.permutation(second, SEQS)
    drawn = drawn.at[order[0]].set(TOK_DEV)
    return drawn.at[order[1]].set(TOK_DEV // 4).astype(jnp.int32)


def shard_levels(own_key, extent, cuts, smallest, largest):
    level = 1.0
    for dim, shards_of in cuts:
        steps = jax.random.uniform(jax.random.fold_in(jax.random.fold_in(own_key, 6), dim), (shards_of,), jnp.float32, smallest / len(cuts), largest / len(cuts))
        level = level * jnp.repeat(jnp.exp(steps), extent[dim] // shards_of).reshape((-1,) + (1,) * (len(extent) - 1 - dim))
    return level


def centred(stream_key, extent, deviation, bound, cuts=(), kind=jnp.bfloat16):
    level = shard_levels(stream_key, extent, cuts, -0.22, 0.18) if cuts else 1.0
    values = jax.random.normal(stream_key, extent, jnp.float32) * deviation * level
    return jnp.minimum(jnp.maximum(values, -bound), bound).astype(kind)


def setup_inputs(seed: int = 0) -> dict:
    arg_keys = jax.random.split(jax.random.key(seed), 20)
    return {
        "tokens": centred(arg_keys[0], (TOKENS, D), 1.0, 6.0, ((0, 128),)),
        "norm_in": jnp.clip(1.0 + 0.1 * jax.random.normal(arg_keys[1], (D,), jnp.float32), 0.5, 1.5).astype(jnp.bfloat16),
        "w_query": centred(arg_keys[2], (D, KDIM), D ** -0.5, 0.1875, ((0, 8),)),
        "w_key": centred(arg_keys[3], (D, KDIM), D ** -0.5, 0.1875, ((0, 8),)),
        "w_value": centred(arg_keys[4], (D, VDIM), D ** -0.5, 0.1875, ((0, 8),)),
        "w_gate_out": centred(arg_keys[5], (D, VDIM), D ** -0.5, 0.1875, ((0, 8),)),
        "w_decay": centred(arg_keys[6], (D, NH), D ** -0.5, 0.1875, ((0, 8),)),
        "w_beta": centred(arg_keys[7], (D, NH), D ** -0.5, 0.1875, ((0, 8),)),
        "decay_log": jnp.clip(-6.0 + 5.0 * jax.random.uniform(arg_keys[8], (NH,), jnp.float32) ** shard_levels(arg_keys[8], (NH,), ((0, 8),), -0.2, 0.2), -6.0, -1.0).astype(jnp.bfloat16),
        "decay_bias": jnp.clip(-2.0 + 3.0 * jax.random.uniform(arg_keys[9], (NH,), jnp.float32) ** shard_levels(arg_keys[9], (NH,), ((0, 8),), -0.2, 0.2), -2.0, 1.0).astype(jnp.bfloat16),
        "conv_weight": centred(arg_keys[10], (CONV, CH), 0.5, 2.0, ((1, 8),)),
        "head_gain": jnp.clip(1.0 + 0.1 * jax.random.normal(arg_keys[11], (DV,), jnp.float32), 0.5, 1.5).astype(jnp.bfloat16),
        "w_output": centred(arg_keys[12], (VDIM, D), VDIM ** -0.5, 0.125, ((0, 8),)),
        "norm_mid": jnp.clip(1.0 + 0.1 * jax.random.normal(arg_keys[13], (D,), jnp.float32), 0.5, 1.5).astype(jnp.bfloat16),
        "w_gate": centred(arg_keys[14], (D, FF), D ** -0.5, 0.1875, ((0, 8),)),
        "w_up": centred(arg_keys[15], (D, FF), D ** -0.5, 0.1875, ((0, 8),)),
        "w_down": centred(arg_keys[16], (FF, D), FF ** -0.5, 0.109375, ((0, 8),)),
        "lengths": draw_lengths(jax.random.fold_in(arg_keys[19], 71), 0),
        "cotangent": centred(arg_keys[18], (TOKENS, D), 1.0, 6.0, ((0, 128),)),
    }


@jax.custom_vjp
def low(v):
    return lax.optimization_barrier(v.astype(jnp.bfloat16)).astype(jnp.float32)

@jax.custom_vjp
def low_back(v):
    return v

def low_keep(v):
    return (low(v), None)

def low_pass(kept, grad):
    return (grad,)

def back_keep(v):
    return (v, None)

def back_low(kept, grad):
    return (low(grad),)
low.defvjp(low_keep, low_pass)
low_back.defvjp(back_keep, back_low)

def matmul(left, right):
    return jnp.dot(left, right, precision=lax.Precision.HIGHEST)

def rms_scale(values, gain):
    return values * lax.rsqrt(lax.optimization_barrier(jnp.mean(values * values, axis=-1, keepdims=True)) + 1e-06) * gain

def unit_rows(values):
    return values * lax.rsqrt(lax.optimization_barrier(jnp.sum(values * values, axis=-1, keepdims=True)) + 1e-06)

def causal_conv(values, kernel):
    length = values.shape[0]
    taps = kernel.shape[0]
    padded = jnp.pad(values, ((taps - 1, 0), (0, 0)))
    total = padded[0:length] * kernel[0]
    for offset in range(1, taps):
        total = total + padded[offset:offset + length] * kernel[offset]
    return total

def span_step(state, pieces):
    queries, keys, values, betas, log_decay = pieces
    highest = lax.Precision.HIGHEST
    width = queries.shape[1]
    position = jnp.arange(width)
    inclusive = (position[:, None] >= position[None, :]).astype(jnp.float32)
    strict = (position[:, None] > position[None, :]).astype(jnp.float32)
    cumulative = jnp.cumsum(log_decay, axis=1)
    spread = cumulative[:, :, None] - cumulative[:, None, :]
    within = jnp.exp(spread * inclusive) * inclusive
    gram = jnp.einsum('hid,hjd->hij', keys, keys, precision=highest)
    system = jnp.eye(width, dtype=jnp.float32) + betas[:, :, None] * gram * within * strict
    lead = jnp.exp(cumulative)[:, :, None]
    weighted_keys = jax.scipy.linalg.solve_triangular(system, betas[:, :, None] * lead * keys, lower=True, unit_diagonal=True)
    weighted_values = jax.scipy.linalg.solve_triangular(system, betas[:, :, None] * values, lower=True, unit_diagonal=True)
    fresh = weighted_values - jnp.einsum('hcd,hvd->hcv', weighted_keys, state, precision=highest)
    carried = jnp.einsum('hcd,hvd->hcv', lead * queries, state, precision=highest)
    scores = jnp.einsum('hid,hjd->hij', queries, keys, precision=highest) * within
    outputs = carried + jnp.einsum('hij,hjv->hiv', scores, fresh, precision=highest)
    final = cumulative[:, -1:]
    tail = jnp.exp(final - cumulative)[:, :, None] * keys
    state = jnp.exp(final)[:, :, None] * state + jnp.einsum('hcv,hcd->hvd', fresh, tail, precision=highest)
    return (state, outputs)

def mixer_core(projected, decay_raw, beta_raw, gate_raw, kernel, decay_log, decay_bias, head_gain):
    length = projected.shape[0]
    blocks = length // SPAN
    convolved = jax.nn.silu(causal_conv(projected, kernel))
    queries = convolved[:, :KDIM].reshape(length, NH, DK)
    keys = convolved[:, KDIM:2 * KDIM].reshape(length, NH, DK)
    values = convolved[:, 2 * KDIM:].reshape(length, NH, DV)
    queries = unit_rows(queries) * DK ** (-0.5)
    keys = unit_rows(keys)
    betas = jax.nn.sigmoid(beta_raw)
    log_decay = -jnp.exp(decay_log) * jax.nn.softplus(decay_raw + decay_bias)

    def blocked(array):
        shaped = array.reshape((blocks, SPAN) + array.shape[1:])
        return jnp.swapaxes(shaped, 1, 2)
    start = jnp.zeros((NH, DV, DK), jnp.float32)
    final, outputs = lax.scan(jax.checkpoint(span_step), start, (blocked(queries), blocked(keys), blocked(values), blocked(betas), blocked(log_decay)))
    outputs = jnp.swapaxes(outputs, 1, 2).reshape(length, NH, DV)
    normed = rms_scale(outputs, head_gain)
    gated = normed * jax.nn.silu(gate_raw).reshape(length, NH, DV)
    return gated.reshape(length, NH * DV)

def layer(sequence, weights):
    norm_in, w_query, w_key, w_value, w_gate_out, w_decay, w_beta, decay_log, decay_bias, conv_weight, head_gain, w_output, norm_mid, w_gate, w_up, w_down = weights
    normed = low(rms_scale(sequence, norm_in))
    projected = low_back(matmul(normed, jnp.concatenate([w_query, w_key, w_value], axis=1)))
    decay_raw = low_back(matmul(normed, w_decay))
    beta_raw = low_back(matmul(normed, w_beta))
    gate_raw = low_back(matmul(normed, w_gate_out))
    mixed = low(mixer_core(projected, decay_raw, beta_raw, gate_raw, conv_weight, decay_log, decay_bias, head_gain))
    branch = low_back(matmul(mixed, w_output))
    resid = sequence + branch
    normed_mid = low(rms_scale(resid, norm_mid))
    gate = low_back(matmul(normed_mid, w_gate))
    upward = low_back(matmul(normed_mid, w_up))
    hidden = low(jax.nn.silu(gate) * upward)
    downward = low_back(matmul(hidden, w_down))
    return resid + downward

def reference(tokens, norm_in, w_query, w_key, w_value, w_gate_out, w_decay, w_beta, decay_log, decay_bias, conv_weight, head_gain, w_output, norm_mid, w_gate, w_up, w_down, lengths, cotangent):
    weights = tuple((item.astype(jnp.float32) for item in (norm_in, w_query, w_key, w_value, w_gate_out, w_decay, w_beta, decay_log, decay_bias, conv_weight, head_gain, w_output, norm_mid, w_gate, w_up, w_down)))
    inputs = tokens.astype(jnp.float32).reshape(SEQS, TOK_DEV, D)
    upstream_all = cotangent.astype(jnp.float32).reshape(SEQS, TOK_DEV, D)

    def one_sequence(totals, item):
        sequence, upstream, length = item
        live = (jnp.arange(TOK_DEV, dtype=jnp.int32) < length).astype(jnp.float32)[:, None]
        result, pull = jax.vjp(layer, sequence, weights)
        sequence_grad, weight_grads = pull(upstream * live)
        totals = jax.tree.map(jnp.add, totals, weight_grads)
        return (totals, (result.astype(jnp.bfloat16), sequence_grad))
    zeros = jax.tree.map(jnp.zeros_like, weights)
    totals, outputs = lax.scan(one_sequence, zeros, (inputs, upstream_all, lengths))
    results, sequence_grads = outputs
    grad_norm_in, grad_query, grad_key, grad_value, grad_gate_out, grad_decay, grad_beta, grad_decay_log, grad_decay_bias, grad_conv, grad_head_gain, grad_output, grad_norm_mid, grad_gate, grad_up, grad_down = totals
    return (results.reshape(TOKENS, D), sequence_grads.reshape(TOKENS, D), grad_norm_in, grad_query, grad_key, grad_value, grad_gate_out, grad_decay, grad_beta, grad_decay_log, grad_decay_bias, grad_conv, grad_head_gain, grad_output, grad_norm_mid, grad_gate, grad_up, grad_down)
```

```python
import functools

import jax
import jax.numpy as jnp
from jax import lax
from jax.sharding import PartitionSpec as P
from jax.experimental import pallas as pl
from jax.experimental.pallas import tpu as pltpu

T = 256
NH = 8
DK = 128
DV = 256
HALF = 3200
EXTRA = 3072
F32 = jnp.float32
BF16 = jnp.bfloat16
NN = (((1,), (0,)), ((), ()))
NT = (((1,), (1,)), ((), ()))
TN = (((0,), (0,)), ((), ()))


def split(a):
    high = a.astype(BF16)
    return high, (a - high.astype(F32)).astype(BF16)


def dot_one(a, b, dims):
    return lax.dot_general(a, b, dims, preferred_element_type=F32)


def dot_three(a, b, dims=NN):
    return (
        dot_one(a[0], b[1], dims) + dot_one(a[1], b[0], dims) + dot_one(a[0], b[0], dims)
    )


def iotas(n=T):
    return (
        lax.broadcasted_iota(jnp.int32, (n, n), 0),
        lax.broadcasted_iota(jnp.int32, (n, n), 1),
    )


def shift_down(values, count):
    if count == 0:
        return values
    row = lax.broadcasted_iota(jnp.int32, values.shape, 0)
    return jnp.where(row >= count, pltpu.roll(values, count, 0), 0.0)


def shift_up(values, count):
    if count == 0:
        return values
    row = lax.broadcasted_iota(jnp.int32, values.shape, 0)
    return jnp.where(row < T - count, pltpu.roll(values, T - count, 0), 0.0)


def sigmoid(v):
    return 1.0 / (1.0 + jnp.exp(-v))


def conv(values, taps):
    total = values * taps[3:4]
    for j in range(3):
        total = total + shift_down(values, 3 - j) * taps[j : j + 1]
    return total


def conv_back(grad, values, taps):
    back = grad * taps[3:4]
    rows = []
    for j in range(3):
        back = back + shift_up(grad, 3 - j) * taps[j : j + 1]
        rows.append(jnp.sum(grad * shift_down(values, 3 - j), axis=0, keepdims=True))
    rows.append(jnp.sum(grad * values, axis=0, keepdims=True))
    rows.append(jnp.zeros((4, grad.shape[1]), F32))
    return back, jnp.concatenate(rows, axis=0)


def unit(values):
    scale = lax.rsqrt(jnp.sum(values * values, axis=-1, keepdims=True) + 1e-06)
    return values * scale, scale


def unit_back(grad, rows, scale):
    return scale * (grad - rows * jnp.sum(grad * rows, axis=-1, keepdims=True))


def to_row(col, same):
    return jnp.sum(jnp.where(same, col, 0.0), axis=0, keepdims=True)


def to_col(row, same):
    return jnp.sum(jnp.where(same, row, 0.0), axis=1, keepdims=True)


def softplus(z):
    return jnp.maximum(z, 0.0) + jnp.log1p(jnp.exp(-jnp.abs(z)))


def prepare(extra, scalars, head, slot):
    lane = lax.broadcasted_iota(jnp.int32, (T, 128), 1)
    decay_raw = jnp.sum(jnp.where(lane == slot, extra, 0.0), axis=1, keepdims=True)
    beta_raw = jnp.sum(jnp.where(lane == slot + 4, extra, 0.0), axis=1, keepdims=True)
    lane1 = lax.broadcasted_iota(jnp.int32, (1, 128), 1)
    decay_log = jnp.sum(jnp.where(lane1 == head, scalars[0:1], 0.0), axis=1, keepdims=True)
    decay_bias = jnp.sum(jnp.where(lane1 == head, scalars[1:2], 0.0), axis=1, keepdims=True)
    z = decay_raw + decay_bias
    rate = jnp.exp(decay_log)
    log_decay = -rate * softplus(z)
    return log_decay, sigmoid(beta_raw), z, rate


def spread_of(log_decay):
    i, j = iotas()
    same = i == j
    total_row = jnp.sum(jnp.where(i <= j, log_decay, 0.0), axis=0, keepdims=True)
    total_col = to_col(total_row, same)
    keep = i >= j
    return jnp.where(keep, jnp.exp(jnp.where(keep, total_col - total_row, 0.0)), 0.0)


def invert(lower):
    i, j = iotas()
    apart = jnp.bitwise_xor(i, j)
    inv = jnp.where(i == j, 1.0, 0.0) - jnp.where(apart == 1, lower, 0.0)
    size = 2
    while size < T:
        part = split(jnp.where((apart >= size) & (apart < 2 * size), lower, 0.0))
        pieces = split(inv)
        inv = inv - dot_three(pieces, split(dot_three(part, pieces)))
        size *= 2
    return inv


def head_parts(pq, pk, pv, extra, cq, ck, cv, scalars, head, slot):
    pre_q, pre_k, pre_v = conv(pq, cq), conv(pk, ck), conv(pv, cv)
    sig_q, sig_k, sig_v = sigmoid(pre_q), sigmoid(pre_k), sigmoid(pre_v)
    uq, rq = unit(pre_q * sig_q)
    uk, rk = unit(pre_k * sig_k)
    values = pre_v * sig_v
    log_decay, beta, z, rate = prepare(extra, scalars, head, slot)
    within = spread_of(log_decay)
    queries = split(uq * (DK**-0.5))
    keys = split(uk)
    gram = dot_three(keys, keys, NT)
    scores = dot_three(queries, keys, NT)
    return (
        (pre_q, pre_k, pre_v),
        (sig_q, sig_k, sig_v),
        (uq, rq, uk, rk, values),
        (log_decay, beta, z, rate),
        within,
        queries,
        keys,
        gram,
        scores,
    )


def forward_head(pq, pk, pv, pg, extra, cq, ck, cv, scalars, gain, head, slot):
    i, j = iotas()
    _, _, (_, _, _, _, values), (_, beta, _, _), within, _, _, gram, scores = head_parts(
        pq, pk, pv, extra, cq, ck, cv, scalars, head, slot
    )
    lower = jnp.where(i > j, beta * gram * within, 0.0)
    inv = invert(lower)
    fresh = dot_three(split(inv), split(beta * values))
    core = dot_three(split(scores * within), split(fresh))
    scale = lax.rsqrt(jnp.mean(core * core, axis=-1, keepdims=True) + 1e-06)
    mixed = core * scale * gain * (pg * sigmoid(pg))
    return mixed, inv, fresh, core


def backward_head(
    pq, pk, pv, pg, extra, cq, ck, cv, scalars, gain, head, slot, grad, inv, fresh, core
):
    i, j = iotas()
    (pre_q, pre_k, pre_v), (sig_q, sig_k, sig_v), units, decays, within, queries, keys, gram, scores = (
        head_parts(pq, pk, pv, extra, cq, ck, cv, scalars, head, slot)
    )
    uq, rq, uk, rk, values = units
    log_decay, beta, z, rate = decays
    scale = lax.rsqrt(jnp.mean(core * core, axis=-1, keepdims=True) + 1e-06)
    normed = core * scale
    sig_g = sigmoid(pg)
    gated = pg * sig_g
    d_gate = grad * normed * gain * (sig_g * (1.0 + pg * (1.0 - sig_g)))
    d_normed = grad * gated
    d_gain = jnp.sum(d_normed * normed, axis=0, keepdims=True)
    d_normed = d_normed * gain
    d_core = scale * (d_normed - normed * jnp.mean(d_normed * normed, axis=-1, keepdims=True))
    weights = scores * within
    d_core2, fresh2 = split(d_core), split(fresh)
    d_weights = dot_three(d_core2, fresh2, NT)
    d_fresh = dot_three(split(weights), d_core2, TN)
    d_base = dot_three(split(inv), split(d_fresh), TN)
    d_system = jnp.where(i > j, -dot_three(split(d_base), fresh2, NT), 0.0)
    d_scores = split(d_weights * within)
    product = gram * within
    d_gram = d_system * (beta * within)
    d_q = dot_three(d_scores, keys)
    d_k = dot_three(d_scores, queries, TN)
    d_gram2 = split(d_gram)
    d_k = d_k + dot_three(d_gram2, keys) + dot_three(d_gram2, keys, TN)
    d_beta = jnp.sum(d_system * product, axis=1, keepdims=True) + jnp.sum(
        d_base * values, axis=1, keepdims=True
    )
    d_values = beta * d_base
    ends = d_weights * weights + d_system * (beta * product)
    same = i == j
    d_total = to_row(jnp.sum(ends, axis=1, keepdims=True), same) - jnp.sum(
        ends, axis=0, keepdims=True
    )
    d_log = jnp.sum(jnp.where(i <= j, d_total, 0.0), axis=1, keepdims=True)
    d_raw = d_log * (-rate * sigmoid(z))
    d_decay_log = jnp.sum(d_log * log_decay, axis=0, keepdims=True)
    d_bias = jnp.sum(d_raw, axis=0, keepdims=True)
    d_beta_raw = d_beta * beta * (1.0 - beta)

    def through(d, pre, sig, proj, taps):
        return conv_back(d * (sig * (1.0 + pre * (1.0 - sig))), proj, taps)

    d_pq, d_cq = through(unit_back(d_q * (DK**-0.5), uq, rq), pre_q, sig_q, pq, cq)
    d_pk, d_ck = through(unit_back(d_k, uk, rk), pre_k, sig_k, pk, ck)
    d_pv, d_cv = through(d_values, pre_v, sig_v, pv, cv)
    return d_pq, d_pk, d_pv, d_gate, d_raw, d_beta_raw, d_cq, d_ck, d_cv, d_gain, d_decay_log, d_bias


def forward_kernel(base, pq, pk, pv, pg, px, cq, ck, cv, sc, gn, *rest):
    mixed, inv, fresh, core = rest[-4:]
    g = base + pl.program_id(0)
    m, x, u, c = forward_head(
        pq[0], pk[0], pv[0], pg[0], px[0], cq[...], ck[...], cv[...], sc[...], gn[...], g, g & 3
    )
    mixed[...] = m.astype(BF16)
    inv[0] = x
    fresh[0] = u
    core[0] = c


def backward_kernel(half, pq, pk, pv, pg, px, cq, ck, cv, sc, gn, grad, inv, fresh, core, *rest):
    out, oq, ok, ov, og, os = rest[-6:]
    slot = pl.program_id(0)
    g = 4 * half + slot
    r = backward_head(
        pq[0], pk[0], pv[0], pg[0], px[0], cq[...], ck[...], cv[...], sc[...], gn[...], g, slot,
        grad[...], inv[0], fresh[0], core[0],
    )
    d_pq, d_pk, d_pv, d_gate, d_raw, d_beta, d_cq, d_ck, d_cv, d_gain, d_log, d_bias = r

    @pl.when(slot == 0)
    def _():
        out[:, EXTRA:] = jnp.zeros((T, 128), BF16)
        og[...] = jnp.zeros_like(og)
        os[...] = jnp.zeros_like(os)

    out[:, pl.ds(pl.multiple_of(slot * 128, 128), 128)] = d_pq.astype(BF16)
    out[:, pl.ds(pl.multiple_of(512 + slot * 128, 128), 128)] = d_pk.astype(BF16)
    out[:, pl.ds(pl.multiple_of(1024 + slot * 256, 256), 256)] = d_pv.astype(BF16)
    out[:, pl.ds(pl.multiple_of(2048 + slot * 256, 256), 256)] = d_gate.astype(BF16)
    lane = lax.broadcasted_iota(jnp.int32, (T, 128), 1)
    old = out[:, EXTRA:].astype(F32)
    out[:, EXTRA:] = jnp.where(
        lane == slot, d_raw, jnp.where(lane == slot + 4, d_beta, old)
    ).astype(BF16)
    oq[...] = d_cq
    ok[...] = d_ck
    ov[...] = d_cv
    og[0:1] += d_gain
    lane1 = lax.broadcasted_iota(jnp.int32, (1, 128), 1)
    os[0:1] += jnp.where(lane1 == g, d_log, 0.0)
    os[1:2] += jnp.where(lane1 == g, d_bias, 0.0)


def common_specs(base):
    def half(g):
        return (base + g) >> 2

    def slot(g):
        return (base + g) & 3

    return [
        pl.BlockSpec((1, T, 128), lambda g: (half(g), 0, slot(g))),
        pl.BlockSpec((1, T, 128), lambda g: (half(g), 0, 4 + slot(g))),
        pl.BlockSpec((1, T, 256), lambda g: (half(g), 0, 4 + slot(g))),
        pl.BlockSpec((1, T, 256), lambda g: (half(g), 0, 8 + slot(g))),
        pl.BlockSpec((1, T, 128), lambda g: (half(g), 0, 24)),
        pl.BlockSpec((4, 128), lambda g: (0, base + g)),
        pl.BlockSpec((4, 128), lambda g: (0, 8 + base + g)),
        pl.BlockSpec((4, 256), lambda g: (0, 8 + base + g)),
        pl.BlockSpec((8, 128), lambda g: (0, 0)),
        pl.BlockSpec((1, 256), lambda g: (0, 0)),
    ]


def wide_spec():
    return pl.BlockSpec((T, DV), lambda g: (0, g))


def head_spec():
    return pl.BlockSpec((1, T, T), lambda g: (g, 0, 0))


def params(heads):
    return dict(
        compiler_params=pltpu.CompilerParams(vmem_limit_bytes=48 << 20),
        cost_estimate=pl.CostEstimate(
            flops=heads * 5 * 10**9, bytes_accessed=heads * (2 << 20), transcendentals=0
        ),
    )


def mixer_forward(base, heads, p, kernel, scalars, gain, deps=()):
    return pl.pallas_call(
        functools.partial(forward_kernel, base),
        grid=(heads,),
        in_specs=common_specs(base) + [pl.BlockSpec(memory_space=pl.ANY)] * len(deps),
        out_specs=[wide_spec(), head_spec(), head_spec(), head_spec()],
        out_shape=[jax.ShapeDtypeStruct((T, heads * DV), BF16)]
        + [jax.ShapeDtypeStruct((heads, T, T), F32)] * 3,
        name="mixer_forward",
        **params(heads),
    )(p, p, p, p, p, kernel, kernel, kernel, scalars, gain, *deps)


def mixer_backward(half, p, kernel, scalars, gain, grad, inv, fresh, core, deps=()):
    shape = jax.ShapeDtypeStruct
    return pl.pallas_call(
        functools.partial(backward_kernel, half),
        grid=(4,),
        in_specs=common_specs(4 * half)
        + [wide_spec(), head_spec(), head_spec(), head_spec()]
        + [pl.BlockSpec(memory_space=pl.ANY)] * len(deps),
        out_specs=[
            pl.BlockSpec((T, HALF), lambda g: (0, 0)),
            pl.BlockSpec((8, 128), lambda g: (0, g)),
            pl.BlockSpec((8, 128), lambda g: (0, g)),
            pl.BlockSpec((8, 256), lambda g: (0, g)),
            pl.BlockSpec((8, 256), lambda g: (0, 0)),
            pl.BlockSpec((8, 128), lambda g: (0, 0)),
        ],
        out_shape=[
            shape((T, HALF), BF16),
            shape((8, 512), F32),
            shape((8, 512), F32),
            shape((8, 1024), F32),
            shape((8, 256), F32),
            shape((8, 128), F32),
        ],
        name="mixer_backward",
        **params(4),
    )(p, p, p, p, p, kernel, kernel, kernel, scalars, gain, grad, inv, fresh, core, *deps)

LINES = 1536


def index(x, y, z, core):
    return ((z * 2 + (x & 1)) * 2 + core) * 8 + y * 2 + (x >> 1)


def route(move):
    pairs = []
    for x in range(4):
        for y in range(4):
            for z in range(4):
                for core in range(2):
                    a, b, c, d = move(x, y, z, core)
                    pairs.append((index(x, y, z, core), index(a % 4, b % 4, c % 4, d)))
    return pairs


Y_UP = route(lambda x, y, z, c: (x, y + 1, z, c))
Y_DOWN = route(lambda x, y, z, c: (x, y - 1, z, c))
Z_UP = route(lambda x, y, z, c: (x, y, z + 1, c))
Z_DOWN = route(lambda x, y, z, c: (x, y, z - 1, c))
Z_FAR = route(lambda x, y, z, c: (x, y, z + 2, c))
X_ACROSS = route(lambda x, y, z, c: (3 - x, y, z, c))
X_BESIDE = route(lambda x, y, z, c: (x ^ 1, y, z, c))
CORE = route(lambda x, y, z, c: (x, y, z, 1 - c))


def send(value, pairs):
    return lax.ppermute(value, ("rep", "shard"), pairs)


def after(value, *others):
    return lax.optimization_barrier((value,) + others)[0]


def pick(array, position):
    return lax.dynamic_index_in_dim(array, position, 0, keepdims=False)


def tie(values, other):
    never = other[0, 0] != other[0, 0]
    return tuple(jnp.where(never, jnp.zeros_like(v), v) for v in values)


def add(*parts):
    total = parts[0].astype(F32)
    for part in parts[1:]:
        total = total + part.astype(F32)
    return total.astype(BF16)


class Place:
    def __init__(self):
        rep, shard = lax.axis_index("rep"), lax.axis_index("shard")
        self.core, self.low, self.z = rep & 1, (rep >> 1) & 1, rep >> 2
        self.y, self.high = shard >> 1, shard & 1
        self.chip = (rep >> 1) * 8 + shard

    def halves(self, mine, other):
        first = self.core == 0
        return jnp.where(first, mine, other), jnp.where(first, other, mine)


def gather_start(own):
    return own, send(own, X_ACROSS), send(own, Y_UP), send(own, Y_DOWN)


def gather_next(parts):
    own, across, below, above = parts
    rows = own.shape[0] // 2
    far = send(below[:rows], Y_UP), send(above[rows:], Y_DOWN)
    return parts + far + (send(across, Y_UP), send(across, Y_DOWN))


def gather_end(parts, place):
    own, across, below, above, far_top, far_low, across_below, across_above = parts
    far = jnp.concatenate([far_top, far_low], axis=0)
    across_far = send(far, X_ACROSS)
    buffer = jnp.zeros((4, 2) + own.shape, own.dtype)
    for step, side, part in (
        (0, 0, own), (0, 1, across), (3, 0, below), (1, 0, above),
        (3, 1, across_below), (1, 1, across_above), (2, 0, far), (2, 1, across_far),
    ):
        start = ((place.y + step) & 3, place.high ^ side) + (0,) * own.ndim
        buffer = lax.dynamic_update_slice(buffer, part[None, None], start)
    return buffer.reshape((8,) + own.shape)


def turn(array, steps):
    width = array.shape[-1] // 4
    double = jnp.concatenate([array, array], axis=-1)
    return lax.dynamic_slice_in_dim(double, (steps & 3) * width, 4 * width, axis=-1)


def ring_sum(chunks, up, down):
    own, above, far, below = chunks
    half = far.shape[0] // 2
    low, high = send(far[:half], up), send(far[half:], down)

    def second():
        first = (
            jnp.concatenate([add(above[:half], low), above[half:]]),
            jnp.concatenate([below[:half], add(below[half:], high)]),
        )

        def third():
            upward, downward = send(first[0], up), send(first[1], down)
            return (upward, downward), lambda: add(own, upward, downward)

        return first, third

    return second


def ring_total(chunks, up, down):
    return ring_sum(chunks, up, down)()[1]()[1]()


def shard_chunks(full, place):
    full = full.reshape((4, 2) + full.shape[1:])
    return [pick(full, (place.y + step) & 3) for step in range(4)]


def across_sum(part, place):
    return add(pick(part, place.high), send(pick(part, place.high ^ 1), X_ACROSS))


def reduce_replicas(part, place):
    part = part.reshape((2, 4) + part.shape[1:])
    near = add(pick(part, place.low), send(pick(part, place.low ^ 1), X_BESIDE))
    z = place.z
    one = add(
        pick(near, z),
        send(pick(near, (z + 1) & 3), Z_UP),
        send(pick(near, (z + 3) & 3), Z_DOWN),
        send(pick(near, (z + 2) & 3), Z_FAR),
    )
    line = jnp.zeros_like(near)
    for step, value in (
        (0, one), (3, send(one, Z_UP)), (1, send(one, Z_DOWN)), (2, send(one, Z_FAR)),
    ):
        line = lax.dynamic_update_slice(
            line, value[None], ((z + step) & 3,) + (0,) * one.ndim
        )
    other = send(line, X_BESIDE)
    first = place.low == 0
    return jnp.concatenate([jnp.where(first, line, other), jnp.where(first, other, line)], axis=0)


def finish_lines(line, place):
    own = ring_total(shard_chunks(line, place), Y_UP, Y_DOWN)
    own = across_sum(own, place)
    own = add(own, send(own, X_BESIDE))
    parts = [own, send(own, Z_DOWN), send(own, Z_FAR), send(own, Z_UP)]
    return turn(jnp.concatenate(parts, axis=-1), -place.z)


def exact_slots(values, place):
    pieces = []
    for _ in range(3):
        pieces.append(lax.reduce_precision(values, 8, 7))
        values = values - pieces[-1]
    mark = (lax.iota(jnp.int32, 64) == place.chip).astype(F32)
    return (mark[None, :, None, None] * jnp.stack(pieces, axis=-1)[:, None]).reshape(8, 128, 3)


def product(left, right):
    return jnp.dot(left, right, preferred_element_type=F32)


def back_product(left, right):
    return lax.dot_general(left, right, NT, preferred_element_type=F32)


def outer_product(left, right):
    return lax.dot_general(left, right, TN, preferred_element_type=F32)


def rms_scale(values, gain):
    return values * lax.rsqrt(jnp.mean(values * values, axis=-1, keepdims=True) + 1e-06) * gain


def gated_unit(gate, upward):
    return jax.nn.silu(gate) * upward


def column(values, rows=128):
    flat = values.reshape(-1)
    return jnp.pad(flat, (0, rows - flat.shape[0]))[:, None]


def local(
    tokens, norm_in, w_query, w_key, w_value, w_gate_out, w_decay, w_beta, decay_log, decay_bias,
    conv_weight, head_gain, w_output, norm_mid, w_gate, w_up, w_down, lengths, cotangent,
):
    place = Place()
    first = place.core == 0
    small = [
        norm_in[:, None], norm_mid[:, None],
        column(jnp.concatenate([head_gain, decay_log, decay_bias])),
        conv_weight.reshape(128, 16), jnp.zeros((128, 101), BF16),
    ]

    def mixer_half(h):
        return jnp.concatenate(
            [
                w_query[:, 512 * h : 512 * h + 512], w_key[:, 512 * h : 512 * h + 512],
                w_value[:, 1024 * h : 1024 * h + 1024], w_gate_out[:, 1024 * h : 1024 * h + 1024],
                w_decay[:, 4 * h : 4 * h + 4], w_beta[:, 4 * h : 4 * h + 4],
            ]
            + small,
            axis=1,
        )

    own_mixer = jnp.where(first, mixer_half(0), mixer_half(1))
    own_down = jnp.concatenate(
        [jnp.where(first, w[:, :512], w[:, 512:]) for w in (w_output, w_down)], axis=0
    )
    own_down = jnp.stack(jnp.split(own_down, 4, axis=1))
    own_up = jnp.where(first, w_gate, w_up)

    mix_parts = gather_next(gather_start(own_mixer))
    line_parts = gather_next(gather_start(pick(own_down, place.z)))
    up_parts = gather_start(after(own_up, mix_parts[-1], mix_parts[-2]))
    mix_m = gather_end(mix_parts, place)
    mix_o = send(mix_m, CORE)
    line = gather_end(line_parts, place)
    line_below, line_above = send(line, Z_UP), send(line, Z_DOWN)

    packed = mix_m[:, :, EXTRA:]
    gain_in = packed[:, :, 8].reshape(1024).astype(F32)
    gain_mid = packed[:, :, 9].reshape(1024).astype(F32)
    shared = packed[:, :, 10].astype(F32)
    gain_head = shared[:, :32].reshape(1, 256)
    scalars = jnp.pad(
        jnp.stack([shared[:, 32], shared[:, 33]]), ((0, 6), (0, 120))
    )
    kernel = packed[:, :, 11:27].reshape(8, 4, 512).swapaxes(0, 1).reshape(4, 4096).astype(F32)
    mix_m, mix_o = mix_m.reshape(1024, HALF), mix_o.reshape(1024, HALF)
    inputs = tokens.astype(F32)
    normed_full, input_pull = jax.vjp(rms_scale, inputs, gain_in)
    normed = normed_full.astype(BF16)
    projected = jnp.stack(place.halves(product(normed, mix_m), product(normed, mix_o)))
    sides = (kernel, scalars, gain_head)
    heads = [mixer_forward(0, 2, projected, *sides)]
    up_parts = gather_next(up_parts[:1] + tie(up_parts[1:], heads[0][0]))
    heads.append(mixer_forward(2, 2, projected, *sides, (heads[0][1],)))
    line_below, line_above = tie((line_below, line_above), heads[1][0])
    line_far = send(line_below[:4], Z_UP), send(line_above[4:], Z_DOWN)
    heads.append(mixer_forward(4, 2, projected, *sides, (heads[1][1],)))
    up_m = gather_end(up_parts[:4] + tie(up_parts[4:], heads[2][0]), place).reshape(1024, 2816)
    up_o = send(up_m, CORE)
    heads.append(mixer_forward(6, 2, projected, *sides, (heads[2][1],)))
    lines = [line, line_above, jnp.concatenate(line_far, axis=0), line_below]
    down_full = jnp.concatenate(lines, axis=-1)
    down_other = send(down_full, CORE)
    mixed = jnp.concatenate([h[0] for h in heads], axis=1)
    saved = [
        [jnp.concatenate([heads[2 * h][i], heads[2 * h + 1][i]]) for i in (1, 2, 3)] for h in (0, 1)
    ]
    out_m, out_o = (w[:, :256].reshape(2048, 512) for w in (down_full, down_other))
    down_m, down_o = (w[:, 256:].reshape(2816, 512) for w in (down_full, down_other))

    def columns(left, mine, other):
        mine, other = (turn(product(left, w), -place.z) for w in (mine, other))
        return jnp.concatenate(place.halves(mine, other), axis=1)

    resid = inputs + columns(mixed, out_m, out_o)
    normed_mid_full, mid_pull = jax.vjp(rms_scale, resid, gain_mid)
    normed_mid = normed_mid_full.astype(BF16)
    gate_pre, up_pre = place.halves(product(normed_mid, up_m), product(normed_mid, up_o))
    active, active_pull = jax.vjp(gated_unit, gate_pre, up_pre)
    hidden = active.astype(BF16)
    block_out = (resid + columns(hidden, down_m, down_o)).astype(BF16)

    positions = jnp.arange(T, dtype=jnp.int32)
    live = (positions < lengths[0]).astype(F32)[:, None]
    grad_out = cotangent.astype(F32) * live
    low_m, low_o = (
        turn(v, place.z) for v in place.halves(*jnp.split(grad_out.astype(BF16), 2, axis=1))
    )
    grad_hidden = back_product(low_m, down_m) + back_product(low_o, down_o)
    grad_gate_pre, grad_up_pre = active_pull(grad_hidden)
    wide_m, wide_o = place.halves(grad_gate_pre.astype(BF16), grad_up_pre.astype(BF16))
    grad_normed_mid = back_product(wide_m, up_m) + back_product(wide_o, up_o)
    grad_resid_part, grad_gain_mid = mid_pull(grad_normed_mid)
    grad_resid = grad_out + grad_resid_part
    grad_branch = grad_resid.astype(BF16)
    branch_m, branch_o = (
        turn(v, place.z) for v in place.halves(*jnp.split(grad_branch, 2, axis=1))
    )

    def paired(left, mine, other):
        width = left.shape[1]
        received = send(jnp.concatenate([left, other], axis=1), CORE)
        return (
            jnp.concatenate([left, received[:, :width]], axis=0),
            jnp.concatenate([mine, received[:, width:]], axis=0),
        )

    def outer(pair):
        return outer_product(*pair).astype(BF16)

    def line_chunks(full):
        return jnp.split(full, 4, axis=-1)

    grad_up_full = outer(paired(normed_mid, wide_m, wide_o)).reshape(8, 128, 2816)
    up_sum = ring_sum(shard_chunks(grad_up_full, place), Y_UP, Y_DOWN)
    grad_down_full = jnp.concatenate(
        [
            outer(paired(mixed, branch_m, branch_o)).reshape(8, 256, 512),
            outer(paired(hidden, low_m, low_o)).reshape(8, 352, 512),
        ],
        axis=1,
    )
    down_sum = ring_sum(line_chunks(grad_down_full), Z_UP, Z_DOWN)

    grad_mixed = back_product(branch_m, out_m) + back_product(branch_o, out_o)
    back0 = mixer_backward(0, projected, *sides, grad_mixed[:, :1024], *saved[0], (grad_up_full,))
    up_first, up_sum = up_sum()
    down_first, down_sum = down_sum()
    back1 = mixer_backward(
        1, projected, *sides, grad_mixed[:, 1024:], *saved[1], (back0[1],) + up_first + down_first
    )
    part_up = up_sum()[1]()
    part_down = down_sum()[1]()

    mine, other = place.halves(back0[0], back1[0])
    mixer_pair = paired(normed, mine, other)
    grad_normed = back_product(mine, mix_m) + back_product(other, mix_o)
    grad_input_part, grad_gain_in = input_pull(grad_normed)
    input_grad = grad_resid + grad_input_part

    grad_kernel = jnp.concatenate([back[i][:4] for i in (1, 2, 3) for back in (back0, back1)], axis=1)
    grad_head_gain = back0[4][0] + back1[4][0]
    grad_scalars = back0[5] + back1[5]
    packed = jnp.concatenate(
        [
            jnp.zeros((8, 128, 8), F32),
            grad_gain_in.reshape(8, 128, 1),
            grad_gain_mid.reshape(8, 128, 1),
            jnp.concatenate(
                [
                    grad_head_gain.reshape(8, 32),
                    jnp.zeros((8, 96), F32),
                ],
                axis=1,
            )[:, :, None],
            grad_kernel.reshape(4, 8, 512).swapaxes(0, 1).reshape(8, 128, 16),
            exact_slots(grad_scalars[:2, :8].T, place),
            jnp.zeros((8, 128, 98), F32),
        ],
        axis=2,
    ).astype(BF16)
    lefts, rights = mixer_pair
    mixer_lines = outer((lefts, turn(rights[:, :LINES], place.z))).reshape(8, 128, LINES)
    mixer_lines = ring_total(line_chunks(mixer_lines), Z_UP, Z_DOWN)
    mixer_rows = outer((lefts, rights[:, LINES:])).reshape(8, 128, HALF - LINES)
    tail = EXTRA - LINES
    mixer_rows = lax.dynamic_update_slice(
        mixer_rows, mixer_rows[:, :, tail:] + packed, (0, 0, tail)
    )
    mixer_rows = ring_total(shard_chunks(mixer_rows, place), Y_UP, Y_DOWN)

    part_up = across_sum(part_up, place)
    part_up = reduce_replicas(part_up.reshape(8, 16, 2816), place).reshape(128, 2816)
    part_down = finish_lines(part_down, place)
    grad_gate, grad_up = (h.astype(F32) for h in place.halves(part_up, send(part_up, CORE)))
    grad_rows = jnp.concatenate(
        [h.astype(F32) for h in place.halves(part_down, send(part_down, CORE))], axis=1
    )

    mixer_lines = finish_lines(mixer_lines, place)
    mixer_rows = across_sum(mixer_rows, place)
    mixer_rows = reduce_replicas(mixer_rows.reshape(8, 16, HALF - LINES), place)
    part = jnp.concatenate([mixer_lines, mixer_rows.reshape(128, HALF - LINES)], axis=1)
    h0, h1 = (h.astype(F32) for h in place.halves(part, send(part, CORE)))

    def both(start, stop):
        return jnp.concatenate([h0[:, start:stop], h1[:, start:stop]], axis=1)

    totals = h0[:, EXTRA:] + h1[:, EXTRA:]
    exact = jnp.sum(totals[:, 27:30].reshape(64, 2, 3), axis=(0, 2))
    return (
        block_out,
        input_grad,
        totals[:, 8],
        both(0, 512),
        both(512, 1024),
        both(1024, 2048),
        both(2048, EXTRA),
        both(EXTRA, EXTRA + 4),
        both(EXTRA + 4, EXTRA + 8),
        exact[:1],
        exact[1:],
        totals[:, 11:27].reshape(4, 512),
        totals[:32, 10],
        grad_rows[:256],
        totals[:, 9],
        grad_gate,
        grad_up,
        grad_rows[256:],
    )


def solution(mesh):
    in_specs = (
        P(("rep", "shard"), None),
        P("shard"),
        P("shard", None),
        P("shard", None),
        P("shard", None),
        P("shard", None),
        P("shard", None),
        P("shard", None),
        P("shard"),
        P("shard"),
        P(None, "shard"),
        P("shard"),
        P("shard", None),
        P("shard"),
        P("shard", None),
        P("shard", None),
        P("shard", None),
        P(("rep", "shard")),
        P(("rep", "shard"), None),
    )
    out_specs = (
        P(("rep", "shard"), None),
        P(("rep", "shard"), None),
        P("shard"),
        P("shard", None),
        P("shard", None),
        P("shard", None),
        P("shard", None),
        P("shard", None),
        P("shard", None),
        P("shard"),
        P("shard"),
        P(None, "shard"),
        P("shard"),
        P("shard", None),
        P("shard"),
        P("shard", None),
        P("shard", None),
        P("shard", None),
    )
    return jax.shard_map(local, mesh=mesh, in_specs=in_specs, out_specs=out_specs, check_vma=False)
```

```python
import jax
import jax.numpy as jnp
from jax import lax
from jax.sharding import PartitionSpec as P
from jax.experimental import pallas as pl
from jax.experimental.pallas import tpu as pltpu

T = 256
NH = 8
DK = 128
DV = 256
HALF = 3200
EXTRA = 3072
LINES = 1536
F32 = jnp.float32
BF16 = jnp.bfloat16
NN = (((1,), (0,)), ((), ()))
NT = (((1,), (1,)), ((), ()))
TN = (((0,), (0,)), ((), ()))


def split(a):
    high = a.astype(BF16)
    return high, (a - high.astype(F32)).astype(BF16)


def dot_one(a, b, dims):
    return lax.dot_general(a, b, dims, preferred_element_type=F32)


def dot_three(a, b, dims=NN):
    return (
        dot_one(a[0], b[1], dims) + dot_one(a[1], b[0], dims) + dot_one(a[0], b[0], dims)
    )


def iotas(n=T):
    return (
        lax.broadcasted_iota(jnp.int32, (n, n), 0),
        lax.broadcasted_iota(jnp.int32, (n, n), 1),
    )


def shift_down(values, count):
    if count == 0:
        return values
    row = lax.broadcasted_iota(jnp.int32, values.shape, 0)
    return jnp.where(row >= count, pltpu.roll(values, count, 0), 0.0)


def shift_up(values, count):
    if count == 0:
        return values
    row = lax.broadcasted_iota(jnp.int32, values.shape, 0)
    return jnp.where(row < T - count, pltpu.roll(values, T - count, 0), 0.0)


def sigmoid(v):
    return 1.0 / (1.0 + jnp.exp(-v))


def conv(values, taps):
    total = values * taps[3:4]
    for j in range(3):
        total = total + shift_down(values, 3 - j) * taps[j : j + 1]
    return total


def conv_back(grad, values, taps):
    back = grad * taps[3:4]
    rows = []
    for j in range(3):
        back = back + shift_up(grad, 3 - j) * taps[j : j + 1]
        rows.append(jnp.sum(grad * shift_down(values, 3 - j), axis=0, keepdims=True))
    rows.append(jnp.sum(grad * values, axis=0, keepdims=True))
    rows.append(jnp.zeros((4, grad.shape[1]), F32))
    return back, jnp.concatenate(rows, axis=0)


def unit(values):
    scale = lax.rsqrt(jnp.sum(values * values, axis=-1, keepdims=True) + 1e-06)
    return values * scale, scale


def unit_back(grad, rows, scale):
    return scale * (grad - rows * jnp.sum(grad * rows, axis=-1, keepdims=True))


def to_row(col, same):
    return jnp.sum(jnp.where(same, col, 0.0), axis=0, keepdims=True)


def to_col(row, same):
    return jnp.sum(jnp.where(same, row, 0.0), axis=1, keepdims=True)


def softplus(z):
    return jnp.maximum(z, 0.0) + jnp.log1p(jnp.exp(-jnp.abs(z)))


def prepare(extra, scalars, head, slot):
    lane = lax.broadcasted_iota(jnp.int32, (T, 128), 1)
    decay_raw = jnp.sum(jnp.where(lane == slot, extra, 0.0), axis=1, keepdims=True)
    beta_raw = jnp.sum(jnp.where(lane == slot + 4, extra, 0.0), axis=1, keepdims=True)
    lane1 = lax.broadcasted_iota(jnp.int32, (1, 128), 1)
    decay_log = jnp.sum(jnp.where(lane1 == head, scalars[0:1], 0.0), axis=1, keepdims=True)
    decay_bias = jnp.sum(jnp.where(lane1 == head, scalars[1:2], 0.0), axis=1, keepdims=True)
    z = decay_raw + decay_bias
    rate = jnp.exp(decay_log)
    log_decay = -rate * softplus(z)
    return log_decay, sigmoid(beta_raw), z, rate


def spread_of(log_decay):
    i, j = iotas()
    same = i == j
    total_row = jnp.sum(jnp.where(i <= j, log_decay, 0.0), axis=0, keepdims=True)
    total_col = to_col(total_row, same)
    keep = i >= j
    return jnp.where(keep, jnp.exp(jnp.where(keep, total_col - total_row, 0.0)), 0.0)


def invert(lowers):
    half = T // 2
    i, j = iotas(half)
    apart = jnp.bitwise_xor(i, j)
    blocks = [low[k : k + half, k : k + half] for low in lowers for k in (0, half)]
    invs = [jnp.where(i == j, 1.0, 0.0) - jnp.where(apart == 1, low, 0.0) for low in blocks]
    size = 2
    while size < half:
        near = (apart >= size) & (apart < 2 * size)
        parts = [split(jnp.where(near, low, 0.0)) for low in blocks]
        pieces = [split(inv) for inv in invs]
        steps = [split(dot_three(part, piece)) for part, piece in zip(parts, pieces)]
        invs = [inv - dot_three(piece, step) for inv, piece, step in zip(invs, pieces, steps)]
        size *= 2
    pieces = [split(inv) for inv in invs]
    steps = [
        split(dot_three(split(low[half:, :half]), pieces[2 * k])) for k, low in enumerate(lowers)
    ]
    zero = jnp.zeros((half, half), F32)
    return [
        jnp.concatenate(
            [
                jnp.concatenate([invs[2 * k], zero], axis=1),
                jnp.concatenate([-dot_three(pieces[2 * k + 1], step), invs[2 * k + 1]], axis=1),
            ],
            axis=0,
        )
        for k, step in enumerate(steps)
    ]


def lockstep(runs):
    runs, results = list(runs), {}
    while len(results) < len(runs):
        for k, run in enumerate(runs):
            if k not in results:
                try:
                    next(run)
                except StopIteration as stop:
                    results[k] = stop.value
    return [results[k] for k in range(len(runs))]


def head_parts(pq, pk, pv, extra, cq, ck, cv, scalars, head, slot):
    pre_q, pre_k, pre_v = conv(pq, cq), conv(pk, ck), conv(pv, cv)
    sig_q, sig_k, sig_v = sigmoid(pre_q), sigmoid(pre_k), sigmoid(pre_v)
    uq, rq = unit(pre_q * sig_q)
    uk, rk = unit(pre_k * sig_k)
    values = pre_v * sig_v
    log_decay, beta, z, rate = prepare(extra, scalars, head, slot)
    within = spread_of(log_decay)
    queries = split(uq * (DK**-0.5))
    keys = split(uk)
    gram = dot_three(keys, keys, NT)
    scores = dot_three(queries, keys, NT)
    return (
        (pre_q, pre_k, pre_v),
        (sig_q, sig_k, sig_v),
        (uq, rq, uk, rk, values),
        (log_decay, beta, z, rate),
        within,
        queries,
        keys,
        gram,
        scores,
    )


def forward_heads(parts, gain):
    i, j = iotas()
    heads = [head_parts(*part[:3], *part[4:]) for part in parts]
    lowers = [jnp.where(i > j, h[3][1] * h[7] * h[4], 0.0) for h in heads]
    invs = invert(lowers)
    freshes = [
        dot_three(split(inv), split(h[3][1] * h[2][4])) for inv, h in zip(invs, heads)
    ]
    cores = [
        dot_three(split(h[8] * h[4]), split(fresh)) for h, fresh in zip(heads, freshes)
    ]
    results = []
    for part, inv, fresh, core in zip(parts, invs, freshes, cores):
        gate = part[3]
        scale = lax.rsqrt(jnp.mean(core * core, axis=-1, keepdims=True) + 1e-06)
        mixed = core * scale * gain * (gate * sigmoid(gate))
        results.append((mixed, inv, fresh, core))
    return results


def backward_head(
    pq, pk, pv, pg, extra, cq, ck, cv, scalars, gain, head, slot, grad, inv, fresh, core
):
    i, j = iotas()
    yield
    (pre_q, pre_k, pre_v), (sig_q, sig_k, sig_v), units, decays, within, queries, keys, gram, scores = (
        head_parts(pq, pk, pv, extra, cq, ck, cv, scalars, head, slot)
    )
    uq, rq, uk, rk, values = units
    log_decay, beta, z, rate = decays
    yield
    scale = lax.rsqrt(jnp.mean(core * core, axis=-1, keepdims=True) + 1e-06)
    normed = core * scale
    sig_g = sigmoid(pg)
    gated = pg * sig_g
    d_gate = grad * normed * gain * (sig_g * (1.0 + pg * (1.0 - sig_g)))
    d_normed = grad * gated
    d_gain = jnp.sum(d_normed * normed, axis=0, keepdims=True)
    d_normed = d_normed * gain
    d_core = scale * (d_normed - normed * jnp.mean(d_normed * normed, axis=-1, keepdims=True))
    yield
    weights = scores * within
    yield
    d_core2, fresh2 = split(d_core), split(fresh)
    d_weights = dot_three(d_core2, fresh2, NT)
    yield
    d_fresh = dot_three(split(weights), d_core2, TN)
    yield
    d_base = dot_three(split(inv), split(d_fresh), TN)
    yield
    d_system = jnp.where(i > j, -dot_three(split(d_base), fresh2, NT), 0.0)
    yield
    d_scores = split(d_weights * within)
    product = gram * within
    d_gram = d_system * (beta * within)
    yield
    d_q = dot_three(d_scores, keys)
    yield
    d_k = dot_three(d_scores, queries, TN)
    d_gram2 = split(d_gram)
    yield
    d_k = d_k + dot_three(d_gram2, keys) + dot_three(d_gram2, keys, TN)
    yield
    d_beta = jnp.sum(d_system * product, axis=1, keepdims=True) + jnp.sum(
        d_base * values, axis=1, keepdims=True
    )
    d_values = beta * d_base
    yield
    ends = d_weights * weights + d_system * (beta * product)
    same = i == j
    d_total = to_row(jnp.sum(ends, axis=1, keepdims=True), same) - jnp.sum(
        ends, axis=0, keepdims=True
    )
    yield
    d_log = jnp.sum(jnp.where(i <= j, d_total, 0.0), axis=1, keepdims=True)
    d_raw = d_log * (-rate * sigmoid(z))
    d_decay_log = jnp.sum(d_log * log_decay, axis=0, keepdims=True)
    d_bias = jnp.sum(d_raw, axis=0, keepdims=True)
    d_beta_raw = d_beta * beta * (1.0 - beta)

    yield
    def through(d, pre, sig, proj, taps):
        return conv_back(d * (sig * (1.0 + pre * (1.0 - sig))), proj, taps)

    yield
    d_pq, d_cq = through(unit_back(d_q * (DK**-0.5), uq, rq), pre_q, sig_q, pq, cq)
    yield
    d_pk, d_ck = through(unit_back(d_k, uk, rk), pre_k, sig_k, pk, ck)
    yield
    d_pv, d_cv = through(d_values, pre_v, sig_v, pv, cv)
    return d_pq, d_pk, d_pv, d_gate, d_raw, d_beta_raw, d_cq, d_ck, d_cv, d_gain, d_decay_log, d_bias


def forward_kernel(core_ref, base, *refs):
    slot = base + pl.program_id(0)
    ins, (mixed_m, mixed_o, inv, fresh, core) = refs[:18], refs[-5:]
    scalars, gain = refs[16][...], refs[17][...]
    parts = [
        [r[...] for r in ins[8 * side : 8 * side + 8]]
        + [scalars, 4 * jnp.bitwise_xor(core_ref[0], side) + slot, slot]
        for side in range(2)
    ]
    for side, (m, x, u, c) in enumerate(forward_heads(parts, gain)):
        (mixed_m, mixed_o)[side][...] = m.astype(BF16)
        inv[0, side] = x
        fresh[0, side] = u
        core[0, side] = c


def backward_kernel(core_ref, base, *refs):
    step = pl.program_id(0)
    slot = base + step
    ins, (inv, fresh, core) = refs[:18], refs[20:23]
    outs = refs[-12:]
    og, os = outs[10:]
    scalars, gain = refs[16][...], refs[17][...]

    @pl.when(step == 0)
    def _():
        for side in range(2):
            outs[5 * side + 1][...] = jnp.zeros((T, 128), BF16)
        og[...] = jnp.zeros_like(og)
        os[...] = jnp.zeros_like(os)

    lane = lax.broadcasted_iota(jnp.int32, (T, 128), 1)
    lane1 = lax.broadcasted_iota(jnp.int32, (1, 128), 1)
    results = lockstep(
        backward_head(
            *[r[...] for r in ins[8 * side : 8 * side + 8]], scalars, gain,
            4 * jnp.bitwise_xor(core_ref[0], side) + slot, slot, refs[18 + side][...],
            inv[0, side], fresh[0, side], core[0, side],
        )
        for side in range(2)
    )
    for side, r in enumerate(results):
        d_pq, d_pk, d_pv, d_gate, d_raw, d_beta, d_cq, d_ck, d_cv, d_gain, d_log, d_bias = r
        out, extra, oq, ok, ov = outs[5 * side : 5 * side + 5]
        head = 4 * jnp.bitwise_xor(core_ref[0], side) + slot
        out[:, pl.ds(pl.multiple_of(step * 128, 128), 128)] = d_pq.astype(BF16)
        out[:, pl.ds(pl.multiple_of(256 + step * 128, 128), 128)] = d_pk.astype(BF16)
        out[:, pl.ds(pl.multiple_of(512 + step * 256, 256), 256)] = d_pv.astype(BF16)
        out[:, pl.ds(pl.multiple_of(1024 + step * 256, 256), 256)] = d_gate.astype(BF16)
        extra[...] = jnp.where(
            lane == slot, d_raw, jnp.where(lane == slot + 4, d_beta, extra[...].astype(F32))
        ).astype(BF16)
        oq[...] = d_cq
        ok[...] = d_ck
        ov[...] = d_cv
        og[0:1] += d_gain
        os[0:1] += jnp.where(lane1 == head, d_log, 0.0)
        os[1:2] += jnp.where(lane1 == head, d_bias, 0.0)


def common_specs(lane):
    base = 2 * lane

    def side(s):
        def head(g, c):
            return 4 * jnp.bitwise_xor(c[0], s) + base + g

        return [
            pl.BlockSpec((T, 128), lambda g, c: (0, 12 * lane + g)),
            pl.BlockSpec((T, 128), lambda g, c: (0, 12 * lane + 2 + g)),
            pl.BlockSpec((T, 256), lambda g, c: (0, 6 * lane + 2 + g)),
            pl.BlockSpec((T, 256), lambda g, c: (0, 6 * lane + 4 + g)),
            pl.BlockSpec((T, 128), lambda g, c: (0, 24)),
            pl.BlockSpec((4, 128), lambda g, c: (0, head(g, c))),
            pl.BlockSpec((4, 128), lambda g, c: (0, 8 + head(g, c))),
            pl.BlockSpec((4, 256), lambda g, c: (0, 8 + head(g, c))),
        ]

    return side(0) + side(1) + [
        pl.BlockSpec((8, 128), lambda g, c: (0, 0)),
        pl.BlockSpec((1, 256), lambda g, c: (0, 0)),
    ]


def sides_of(p_m, p_o, kernel, scalars, gain):
    k = (kernel, kernel, kernel)
    return (p_m,) * 5 + k + (p_o,) * 5 + k + (scalars, gain)


def saved_spec():
    return pl.BlockSpec((1, 2, T, T), lambda g, c: (g, 0, 0, 0))


def params(flops):
    return dict(
        compiler_params=pltpu.CompilerParams(vmem_limit_bytes=48 << 20),
        cost_estimate=pl.CostEstimate(
            flops=flops, bytes_accessed=8 << 20, transcendentals=0
        ),
    )


def mixer_forward(lane, place, sides, deps=()):
    shape = jax.ShapeDtypeStruct
    return pl.pallas_call(
        lambda core, *refs: forward_kernel(core, 2 * lane, *refs),
        grid_spec=pltpu.PrefetchScalarGridSpec(
            num_scalar_prefetch=1,
            grid=(2,),
            in_specs=common_specs(lane) + [pl.BlockSpec(memory_space=pl.ANY)] * len(deps),
            out_specs=[pl.BlockSpec((T, DV), lambda g, c: (0, g))] * 2 + [saved_spec()] * 3,
        ),
        out_shape=[shape((T, 2 * DV), BF16)] * 2 + [shape((2, 2, T, T), F32)] * 3,
        name="mixer_forward",
        **params(20 * 10**9),
    )(place.core_array, *sides_of(*sides), *deps)


def mixer_backward(lane, place, sides, grads, saved, deps=()):
    shape = jax.ShapeDtypeStruct
    rows = [
        pl.BlockSpec((T, LINES), lambda g, c: (0, 0)),
        pl.BlockSpec((T, 128), lambda g, c: (0, 0)),
        pl.BlockSpec((8, 128), lambda g, c: (0, g)),
        pl.BlockSpec((8, 128), lambda g, c: (0, g)),
        pl.BlockSpec((8, 256), lambda g, c: (0, g)),
    ]
    shapes = [
        shape((T, LINES), BF16), shape((T, 128), BF16),
        shape((8, 256), F32), shape((8, 256), F32), shape((8, 512), F32),
    ]
    return pl.pallas_call(
        lambda core, *refs: backward_kernel(core, 2 * lane, *refs),
        grid_spec=pltpu.PrefetchScalarGridSpec(
            num_scalar_prefetch=1,
            grid=(2,),
            in_specs=common_specs(lane)
            + [pl.BlockSpec((T, DV), lambda g, c: (0, 2 * lane + g))] * 2
            + [saved_spec()] * 3
            + [pl.BlockSpec(memory_space=pl.ANY)] * len(deps),
            out_specs=rows * 2
            + [pl.BlockSpec((8, 256), lambda g, c: (0, 0)), pl.BlockSpec((8, 128), lambda g, c: (0, 0))],
        ),
        out_shape=shapes * 2 + [shape((8, 256), F32), shape((8, 128), F32)],
        name="mixer_backward",
        **params(20 * 10**9),
    )(place.core_array, *sides_of(*sides), *grads, *saved, *deps)

def index(x, y, z, core):
    return ((z * 2 + (x & 1)) * 2 + core) * 8 + y * 2 + (x >> 1)


def route(move):
    pairs = []
    for x in range(4):
        for y in range(4):
            for z in range(4):
                for core in range(2):
                    a, b, c, d = move(x, y, z, core)
                    pairs.append((index(x, y, z, core), index(a % 4, b % 4, c % 4, d)))
    return pairs


Y_UP = route(lambda x, y, z, c: (x, y + 1, z, c))
Y_DOWN = route(lambda x, y, z, c: (x, y - 1, z, c))
Y_FAR = route(lambda x, y, z, c: (x, y + 2, z, c))
Z_UP = route(lambda x, y, z, c: (x, y, z + 1, c))
Z_DOWN = route(lambda x, y, z, c: (x, y, z - 1, c))
Z_FAR = route(lambda x, y, z, c: (x, y, z + 2, c))
X_ACROSS = route(lambda x, y, z, c: (3 - x, y, z, c))
X_BESIDE = route(lambda x, y, z, c: (x ^ 1, y, z, c))
X_FAR = route(lambda x, y, z, c: (x ^ 2, y, z, c))
CORE = route(lambda x, y, z, c: (x, y, z, 1 - c))
X_CORE = route(lambda x, y, z, c: (x ^ 1, y, z, 1 - c))


def send(value, pairs):
    return lax.ppermute(value, ("rep", "shard"), pairs)


def together(*groups):
    flat = lax.optimization_barrier(tuple(v for g in groups for v in g))
    result, start = [], 0
    for g in groups:
        result.append(tuple(flat[start : start + len(g)]))
        start += len(g)
    return result


def pick(array, position):
    return lax.dynamic_index_in_dim(array, position, 0, keepdims=False)


def add(*parts):
    total = parts[0].astype(F32)
    for part in parts[1:]:
        total = total + part.astype(F32)
    return total.astype(BF16)


def add_pairs(a, b, c, d):
    return ((a.astype(F32) + b.astype(F32)) + (c.astype(F32) + d.astype(F32))).astype(BF16)


class Place:
    def __init__(self):
        rep, shard = lax.axis_index("rep"), lax.axis_index("shard")
        self.core, self.low, self.z = rep & 1, (rep >> 1) & 1, rep >> 2
        self.y, self.high = shard >> 1, shard & 1
        self.chip = (rep >> 1) * 8 + shard
        self.core_array = self.core.astype(jnp.int32).reshape(1)

    def halves(self, mine, other):
        first = self.core == 0
        return jnp.where(first, mine, other), jnp.where(first, other, mine)


def gather_start(own):
    return own, send(own, X_ACROSS), send(own, Y_UP), send(own, Y_DOWN)


def gather_next(parts):
    own, across, below, above = parts
    rows = own.shape[0] // 2
    far = send(below[:rows], Y_UP), send(above[rows:], Y_DOWN)
    return parts + far + (send(across, Y_UP), send(across, Y_DOWN))


def gather_last(parts):
    far = jnp.concatenate(parts[4:6], axis=0)
    return parts[:4] + parts[6:] + (far, send(far, X_ACROSS))


def gather_end(parts, place):
    own, across, below, above, across_below, across_above, far, across_far = parts
    buffer = jnp.zeros((4, 2) + own.shape, own.dtype)
    for step, side, part in (
        (0, 0, own), (0, 1, across), (3, 0, below), (1, 0, above),
        (3, 1, across_below), (1, 1, across_above), (2, 0, far), (2, 1, across_far),
    ):
        start = ((place.y + step) & 3, place.high ^ side) + (0,) * own.ndim
        buffer = lax.dynamic_update_slice(buffer, part[None, None], start)
    return buffer.reshape((8,) + own.shape)


def turn(array, steps):
    width = array.shape[-1] // 4
    double = jnp.concatenate([array, array], axis=-1)
    return lax.dynamic_slice_in_dim(double, (steps & 3) * width, 4 * width, axis=-1)


def ring_start(chunks, up, down):
    far = chunks[2]
    half = far.shape[0] // 2
    return send(far[:half], up), send(far[half:], down)


def ring_next(chunks, received, up, down):
    _, above, _, below = chunks
    half = above.shape[0] // 2
    low, high = received
    upward = jnp.concatenate([add(above[:half], low), above[half:]])
    downward = jnp.concatenate([below[:half], add(below[half:], high)])
    return send(upward, up), send(downward, down)


def shard_chunks(full, place):
    full = full.reshape((4, 2) + full.shape[1:])
    return [pick(full, (place.y + step) & 3) for step in range(4)]


def line_chunks(full):
    return jnp.split(full, 4, axis=-1)


def row_sum(own, place):
    quarters = own.reshape((2, 2, own.shape[1] // 2) + own.shape[2:])

    def quarter(side, beside):
        return pick(pick(quarters, place.high ^ side), place.low ^ beside)

    return add_pairs(
        quarter(0, 0),
        send(quarter(0, 1), X_BESIDE),
        send(quarter(1, 1), X_ACROSS),
        send(quarter(1, 0), X_FAR),
    )


def row_total(part):
    return add_pairs(part, send(part, Z_FAR), send(part, Z_UP), send(part, Z_DOWN))


def row_spread(part, place):
    beside, core, both = send(part, X_BESIDE), send(part, CORE), send(part, X_CORE)
    first = place.low == 0

    def rows(mine, other):
        return jnp.concatenate([jnp.where(first, mine, other), jnp.where(first, other, mine)])

    return place.halves(rows(part, beside), rows(core, both))


def line_sum(line, place):
    chunks = shard_chunks(line, place)
    return add_pairs(
        chunks[0], send(chunks[2], Y_FAR), send(chunks[1], Y_UP), send(chunks[3], Y_DOWN)
    )


def line_total(own, place):
    keep, give = pick(own, place.high), pick(own, place.high ^ 1)
    return add_pairs(keep, send(keep, X_BESIDE), send(give, X_ACROSS), send(give, X_FAR))


def line_spread(own, place):
    parts = [own, send(own, Z_DOWN), send(own, Z_FAR), send(own, Z_UP)]
    line = turn(jnp.concatenate(parts, axis=-1), -place.z)
    return place.halves(line, send(line, CORE))


def exact_slots(values, place):
    pieces = []
    for _ in range(3):
        pieces.append(lax.reduce_precision(values, 8, 7))
        values = values - pieces[-1]
    mark = (lax.iota(jnp.int32, 64) == place.chip).astype(F32)
    return (mark[None, :, None, None] * jnp.stack(pieces, axis=-1)[:, None]).reshape(8, 128, 3)


def product(left, right):
    return jnp.dot(left, right, preferred_element_type=F32)


def back_product(left, right):
    return lax.dot_general(left, right, NT, preferred_element_type=F32)


def outer_product(left, right):
    return lax.dot_general(left, right, TN, preferred_element_type=F32)


def rms_scale(values, gain):
    return values * lax.rsqrt(jnp.mean(values * values, axis=-1, keepdims=True) + 1e-06) * gain


def gated_unit(gate, upward):
    return jax.nn.silu(gate) * upward


def column(values, rows=128):
    flat = values.reshape(-1)
    return jnp.pad(flat, (0, rows - flat.shape[0]))[:, None]


def local(
    tokens, norm_in, w_query, w_key, w_value, w_gate_out, w_decay, w_beta, decay_log, decay_bias,
    conv_weight, head_gain, w_output, norm_mid, w_gate, w_up, w_down, lengths, cotangent,
):
    place = Place()
    first = place.core == 0
    small = [
        norm_in[:, None], norm_mid[:, None],
        column(jnp.concatenate([head_gain, decay_log, decay_bias])),
        conv_weight.reshape(128, 16), jnp.zeros((128, 101), BF16),
    ]

    def mixer_half(h):
        pieces = []
        for start in (4 * h, 4 * h + 2):
            pieces += [w[:, 128 * start : 128 * start + 256] for w in (w_query, w_key)]
            pieces += [w[:, 256 * start : 256 * start + 512] for w in (w_value, w_gate_out)]
        pieces += [w_decay[:, 4 * h : 4 * h + 4], w_beta[:, 4 * h : 4 * h + 4]]
        return jnp.concatenate(pieces + small, axis=1)

    own_mixer = jnp.where(first, mixer_half(0), mixer_half(1))
    own_down = jnp.concatenate(
        [jnp.where(first, w[:, :512], w[:, 512:]) for w in (w_output, w_down)], axis=0
    )
    own_down = jnp.stack(jnp.split(own_down, 4, axis=1))
    own_up = jnp.where(first, w_gate, w_up)

    mix_parts, line_parts = together(
        gather_start(own_mixer), gather_start(pick(own_down, place.z))
    )
    mix_parts, line_parts = together(gather_next(mix_parts), gather_next(line_parts))
    mix_parts, line_parts = together(gather_last(mix_parts), gather_last(line_parts))
    mix_m = gather_end(mix_parts, place)
    mix_o = send(mix_m, CORE)
    line = gather_end(line_parts, place)
    line_ends = send(line, Z_UP), send(line, Z_DOWN)
    up_parts = gather_start(together((own_up,), mix_parts[-1:])[0][0])

    packed = mix_m[:, :, EXTRA:]
    gain_in = packed[:, :, 8].reshape(1024).astype(F32)
    gain_mid = packed[:, :, 9].reshape(1024).astype(F32)
    shared = packed[:, :, 10].astype(F32)
    gain_head = shared[:, :32].reshape(1, 256)
    scalars = jnp.pad(
        jnp.stack([shared[:, 32], shared[:, 33]]), ((0, 6), (0, 120))
    )
    kernel = packed[:, :, 11:27].reshape(8, 4, 512).swapaxes(0, 1).reshape(4, 4096).astype(F32)
    mix_m, mix_o = mix_m.reshape(1024, HALF), mix_o.reshape(1024, HALF)
    inputs = tokens.astype(F32)
    normed_full, input_pull = jax.vjp(rms_scale, inputs, gain_in)
    normed = normed_full.astype(BF16)
    projected = product(normed, mix_m), product(normed, mix_o)
    sides = projected + (kernel, scalars, gain_head)
    up_parts, sides = together(up_parts, sides)
    up_parts = gather_next(up_parts)
    fore0 = mixer_forward(0, place, sides)
    up_parts, line_ends, fore0 = together(up_parts, line_ends, fore0)
    up_parts = gather_last(up_parts)
    line_far = send(line_ends[0][:4], Z_UP), send(line_ends[1][4:], Z_DOWN)
    fore1 = mixer_forward(1, place, sides, (fore0[2],))
    up_parts, line_far, fore1 = together(up_parts, line_far, fore1)
    lines = [line, line_ends[1], jnp.concatenate(line_far, axis=0), line_ends[0]]
    out_m = jnp.concatenate([v[:, :256] for v in lines], axis=-1).reshape(2048, 512)
    down_m = jnp.concatenate([v[:, 256:] for v in lines], axis=-1).reshape(2816, 512)
    out_o, down_o = send(out_m, CORE), send(down_m, CORE)
    up_m = gather_end(up_parts, place).reshape(1024, 2816)
    up_o = send(up_m, CORE)
    mixed = jnp.concatenate(
        place.halves(
            jnp.concatenate([fore0[0], fore1[0]], axis=1),
            jnp.concatenate([fore0[1], fore1[1]], axis=1),
        ),
        axis=1,
    )

    def columns(left, mine, other):
        mine, other = (turn(product(left, w), -place.z) for w in (mine, other))
        return jnp.concatenate(place.halves(mine, other), axis=1)

    resid = inputs + columns(mixed, out_m, out_o)
    normed_mid_full, mid_pull = jax.vjp(rms_scale, resid, gain_mid)
    normed_mid = normed_mid_full.astype(BF16)
    gate_pre, up_pre = place.halves(product(normed_mid, up_m), product(normed_mid, up_o))
    active, active_pull = jax.vjp(gated_unit, gate_pre, up_pre)
    hidden = active.astype(BF16)
    block_out = (resid + columns(hidden, down_m, down_o)).astype(BF16)

    positions = jnp.arange(T, dtype=jnp.int32)
    live = (positions < lengths[0]).astype(F32)[:, None]
    grad_out = cotangent.astype(F32) * live
    low_m, low_o = (
        turn(v, place.z) for v in place.halves(*jnp.split(grad_out.astype(BF16), 2, axis=1))
    )
    grad_hidden = back_product(low_m, down_m) + back_product(low_o, down_o)
    grad_gate_pre, grad_up_pre = active_pull(grad_hidden)
    wide_m, wide_o = place.halves(grad_gate_pre.astype(BF16), grad_up_pre.astype(BF16))
    grad_normed_mid = back_product(wide_m, up_m) + back_product(wide_o, up_o)
    grad_resid_part, grad_gain_mid = mid_pull(grad_normed_mid)
    grad_resid = grad_out + grad_resid_part
    grad_branch = grad_resid.astype(BF16)
    branch_m, branch_o = (
        turn(v, place.z) for v in place.halves(*jnp.split(grad_branch, 2, axis=1))
    )

    def paired(left, mine, other):
        width = left.shape[1]
        received = send(jnp.concatenate([left, other], axis=1), CORE)
        return (
            jnp.concatenate([left, received[:, :width]], axis=0),
            jnp.concatenate([mine, received[:, width:]], axis=0),
        )

    def outer(lefts, rights):
        return outer_product(lefts, rights).astype(BF16)

    up_chunks = shard_chunks(outer(*paired(normed_mid, wide_m, wide_o)).reshape(8, 128, 2816), place)
    up_sum = ring_start(up_chunks, Y_UP, Y_DOWN)
    down_chunks = line_chunks(
        jnp.concatenate(
            [
                outer(*paired(mixed, branch_m, branch_o)).reshape(8, 256, 512),
                outer(*paired(hidden, low_m, low_o)).reshape(8, 352, 512),
            ],
            axis=1,
        )
    )
    down_sum = ring_start(down_chunks, Z_UP, Z_DOWN)

    grad_mixed = back_product(branch_m, out_m) + back_product(branch_o, out_o)
    grad_mixed = place.halves(grad_mixed[:, :1024], grad_mixed[:, 1024:])
    back0 = mixer_backward(0, place, sides, grad_mixed, fore0[2:], (up_chunks[2], down_chunks[2]))
    up_sum, down_sum, back0, grad_mixed = together(up_sum, down_sum, back0, grad_mixed)
    up_sum = ring_next(up_chunks, up_sum, Y_UP, Y_DOWN)
    down_sum = ring_next(down_chunks, down_sum, Z_UP, Z_DOWN)
    normed_pair, first_pair = paired(normed, back0[0], back0[5])
    first_chunks = outer(normed_pair, turn(first_pair, place.z)).reshape(8, 128, LINES)
    first_chunks = line_chunks(first_chunks)
    first_sum = ring_start(first_chunks, Z_UP, Z_DOWN)
    back1 = mixer_backward(1, place, sides, grad_mixed, fore1[2:], (first_chunks[2],))
    up_sum, down_sum, first_sum, back1 = together(up_sum, down_sum, first_sum, back1)
    first_sum = ring_next(first_chunks, first_sum, Z_UP, Z_DOWN)

    up_part = row_sum(add(up_chunks[0], *up_sum), place)
    down_part = line_sum(add(down_chunks[0], *down_sum), place)

    extra_m, extra_o = back0[1] + back1[1], back0[6] + back1[6]
    second_m = jnp.concatenate([back1[0], extra_m], axis=1)
    second_o = jnp.concatenate([back1[5], extra_o], axis=1)
    second_pair = jnp.concatenate([second_m, send(second_o, CORE)], axis=0)
    grad_normed = (
        back_product(back0[0], mix_m[:, :LINES])
        + back_product(back0[5], mix_o[:, :LINES])
        + back_product(second_m, mix_m[:, LINES:])
        + back_product(second_o, mix_o[:, LINES:])
    )
    grad_input_part, grad_gain_in = input_pull(grad_normed)
    input_grad = grad_resid + grad_input_part

    def taps(i):
        return place.halves(
            jnp.concatenate([back0[i][:4], back1[i][:4]], axis=1),
            jnp.concatenate([back0[i + 5][:4], back1[i + 5][:4]], axis=1),
        )

    grad_kernel = jnp.concatenate(taps(2) + taps(3) + taps(4), axis=1)
    grad_head_gain = back0[10][0] + back1[10][0]
    grad_scalars = back0[11] + back1[11]
    packed = jnp.concatenate(
        [
            jnp.zeros((8, 128, 8), F32),
            grad_gain_in.reshape(8, 128, 1),
            grad_gain_mid.reshape(8, 128, 1),
            jnp.concatenate(
                [
                    grad_head_gain.reshape(8, 32),
                    jnp.zeros((8, 96), F32),
                ],
                axis=1,
            )[:, :, None],
            grad_kernel.reshape(4, 8, 512).swapaxes(0, 1).reshape(8, 128, 16),
            exact_slots(grad_scalars[:2, :8].T, place),
            jnp.zeros((8, 128, 98), F32),
        ],
        axis=2,
    ).astype(BF16)
    (up_part, down_part), first_sum, (packed, normed_pair, second_pair) = together(
        (up_part, down_part), first_sum, (packed, normed_pair, second_pair)
    )
    second_chunks = outer(normed_pair, second_pair).reshape(8, 128, HALF - LINES)
    second_chunks = lax.dynamic_update_slice(
        second_chunks, second_chunks[:, :, LINES:] + packed, (0, 0, LINES)
    )
    second_chunks = shard_chunks(second_chunks, place)
    second_sum = ring_start(second_chunks, Y_UP, Y_DOWN)
    up_part = row_total(up_part)
    second_sum, (up_part,), first_sum = together(second_sum, (up_part,), first_sum)
    second_sum = ring_next(second_chunks, second_sum, Y_UP, Y_DOWN)
    first_part = line_sum(add(first_chunks[0], *first_sum), place)
    second_sum, (first_part, down_part) = together(second_sum, (first_part, down_part))
    second_part = row_sum(add(second_chunks[0], *second_sum), place)
    first_part = line_total(first_part, place)
    down_part = line_total(down_part, place)
    second_part, first_part, down_part, up_part = together(
        (second_part, first_part, down_part, up_part)
    )[0]
    second_part = row_total(second_part)
    first_halves = line_spread(first_part, place)
    second_part, *first_halves = together((second_part,) + first_halves)[0]
    first_halves = [h.astype(F32) for h in first_halves]
    second_halves = [h.astype(F32) for h in row_spread(second_part, place)]
    grad_gate, grad_up = (h.astype(F32) for h in row_spread(up_part, place))
    down_halves = line_spread(down_part, place)
    grad_rows = jnp.concatenate([h.astype(F32) for h in down_halves], axis=1)
    def both(start, stop):
        pieces = [h[:, start:stop] for f, s in zip(first_halves, second_halves) for h in (f, s)]
        return jnp.concatenate(pieces, axis=1)

    def ends(start, stop):
        return jnp.concatenate(
            [h[:, LINES + start : LINES + stop] for h in second_halves], axis=1
        )

    totals = second_halves[0][:, LINES:] + second_halves[1][:, LINES:]
    exact = jnp.sum(totals[:, 27:30].reshape(64, 2, 3), axis=(0, 2))
    return (
        block_out,
        input_grad,
        totals[:, 8],
        both(0, 256),
        both(256, 512),
        both(512, 1024),
        both(1024, 1536),
        ends(0, 4),
        ends(4, 8),
        exact[:1],
        exact[1:],
        totals[:, 11:27].reshape(4, 512),
        totals[:32, 10],
        grad_rows[:256],
        totals[:, 9],
        grad_gate,
        grad_up,
        grad_rows[256:],
    )


def solution(mesh):
    in_specs = (
        P(("rep", "shard"), None),
        P("shard"),
        P("shard", None),
        P("shard", None),
        P("shard", None),
        P("shard", None),
        P("shard", None),
        P("shard", None),
        P("shard"),
        P("shard"),
        P(None, "shard"),
        P("shard"),
        P("shard", None),
        P("shard"),
        P("shard", None),
        P("shard", None),
        P("shard", None),
        P(("rep", "shard")),
        P(("rep", "shard"), None),
    )
    out_specs = (
        P(("rep", "shard"), None),
        P(("rep", "shard"), None),
        P("shard"),
        P("shard", None),
        P("shard", None),
        P("shard", None),
        P("shard", None),
        P("shard", None),
        P("shard", None),
        P("shard"),
        P("shard"),
        P(None, "shard"),
        P("shard"),
        P("shard", None),
        P("shard"),
        P("shard", None),
        P("shard", None),
        P("shard", None),
    )
    return jax.shard_map(local, mesh=mesh, in_specs=in_specs, out_specs=out_specs, check_vma=False)
```
